32 devices in a mesh: slab: 8 (over z, y), rows: 4 (over x, core).
Axes of the slice: x: 2, y: 2, z: 4, core: 2. Of those that a mesh axis runs over, the one named last changes fastest.
Arguments:
- frames: bfloat16 [128, 16, 128, 256], P('slab', 'rows'), may hold values from -6 to 6
- clip_ids: int32 [128], P('slab'), may hold values from 0 to 15, never falling along the last dimension, each value on 1 to 32 neighbouring positions
- norm_gain: float32 [256], replicated, may hold values from 0.1 to 1.9
- norm_shift: float32 [256], replicated, may hold values from -3 to 3
- w_spatial: bfloat16 [3, 3, 256, 256], replicated, may hold values from -0.125 to 0.125
- b_spatial: float32 [256], replicated, may hold values from -3 to 3
- w_time: bfloat16 [3, 256, 256], replicated, may hold values from -0.25 to 0.25
- b_time: float32 [256], replicated, may hold values from -3 to 3
- w_lift: bfloat16 [256, 512], replicated, may hold values from -0.375 to 0.375
- pack_dest: int32 [128], P('slab'), may hold values from 0 to 127, as said below
Outputs:
- packed: bfloat16 [128, 16, 128, 512], P('slab', 'rows')
The draws below stay inside these ranges and needn't reach their ends.
Inputs may be any that keep to these rules, and one draw needn't show every extreme that they name: `clip_ids`: clip ids never fall and each of the 16 clips has at least one frame. pack_dest is a permutation of the frames; from each aligned block of 16 frames exactly 2 land in each aligned block of 16 positions.
All inputs are finite; a program needn't handle non-finite values.
Results may differ from the reference program's by a relative error of at most 0.0056.
Values may be sent and summed in bfloat16 or wider, within the bound.
A program may use at most 192 MiB of HBM per device.

```python
import math
import jax
import jax.numpy as jnp
import numpy as np
from jax import lax

CH = 256
CH_OUT = 512
GROUPS = 32
CLIPS = 16
TF = 16
WIDTH = 128
NFRAMES = 128
HEIGHT = 16


def draw_pack_dest(key, part):
    shards = NFRAMES // TF
    per_peer = TF // shards
    key_off = jax.random.fold_in(key, 11)
    key_src = jax.random.fold_in(key, 12)
    key_dst = jax.random.fold_in(key, 13)
    offsets = jax.random.permutation(key_off, shards).astype(jnp.int32)
    slot = jnp.arange(TF, dtype=jnp.int32)
    source = jnp.arange(shards, dtype=jnp.int32)
    src_perm = jax.vmap(lambda k: jax.random.permutation(k, TF))(jax.random.split(key_src, shards)).astype(jnp.int32)
    dst_perm = jax.vmap(lambda k: jax.random.permutation(k, TF))(jax.random.split(key_dst, shards)).astype(jnp.int32)
    target = (source[:, None] + offsets[slot // per_peer][None, :]) % shards
    arrival = source[:, None] * per_peer + (slot % per_peer)[None, :]
    position = target * TF + dst_perm[target, arrival]
    local = source[:, None] * TF + src_perm
    dest = jnp.zeros((NFRAMES,), jnp.int32).at[local.reshape(-1)].set(position.reshape(-1).astype(jnp.int32))
    return dest


def level_of(key, shape, pieces, least, high):
    loudness = 1.0
    for axis_at, blocks in pieces:
        draws = jax.random.uniform(jax.random.fold_in(jax.random.fold_in(key, 6), axis_at), (blocks,), jnp.float32, least / len(pieces), high / len(pieces))
        loudness = loudness * jnp.repeat(jnp.exp(draws), shape[axis_at] // blocks).reshape((-1,) + (1,) * (len(shape) - 1 - axis_at))
    return loudness


def profile(amount, total, limit, slope):
    loads = [(1 << 20) // math.isqrt(standing ** slope) + 1 for standing in range(2, amount + 1)]
    surplus, given = total - limit - (amount - 1), [1] * (amount - 1)
    while surplus > 0:
        free = [i for i in range(amount - 1) if given[i] < limit]
        mass, left = sum([loads[i] for i in free]), surplus
        for i in free:
            more = min(limit - given[i], max(1, left * loads[i] // mass), surplus)
            given[i] = given[i] + more
            surplus = surplus - more
    return np.array([limit] + given)


def ragged_sizes(stream_key, amount, total, limit, skew):
    if amount == 2:
        one = jax.random.randint(stream_key, (), max(1, total - limit), min(limit, total - 1) + 1)
        return jnp.stack([one, total - one])
    tallies = jnp.asarray(profile(amount, total, limit, skew), jnp.int32)
    twos = (amount - 1) // 2
    source_of, receiver = tallies[1:1 + 2 * twos:2], tallies[2:2 + 2 * twos:2]
    slack = jnp.minimum(source_of - 1, limit - receiver)
    moved = jax.random.randint(jax.random.fold_in(stream_key, 1), (twos,), 0, 1 << 20) % (slack + 1)
    tallies = tallies.at[1:1 + 2 * twos:2].set(source_of - moved).at[2:2 + 2 * twos:2].set(receiver + moved)
    return tallies[jax.random.permutation(jax.random.fold_in(stream_key, 2), amount)]


def bell_draw(stream_key, shape, spread, reach, cuts=(), held_as=jnp.bfloat16):
    loudness = level_of(stream_key, shape, cuts, -0.22, 0.18) if cuts else 1.0
    array = jax.random.normal(stream_key, shape, jnp.float32) * spread * loudness
    return jnp.minimum(jnp.maximum(array, -reach), reach).astype(held_as)


def setup_inputs(seed: int = 0) -> dict:
    arg_keys = jax.random.split(jax.random.key(seed), 11)
    return {
        "frames": bell_draw(arg_keys[0], (NFRAMES, HEIGHT, WIDTH, CH), 1.0, 6.0, ((0, 8), (1, 4))),
        "clip_ids": jnp.searchsorted(jnp.cumsum(ragged_sizes(arg_keys[1], CLIPS, NFRAMES, NFRAMES // 4, 2)), jnp.arange(NFRAMES), side="right").astype(jnp.int32),
        "norm_gain": jnp.clip(1.0 + 0.18 * jax.random.normal(arg_keys[2], (CH,), jnp.float32), 0.1, 1.9),
        "norm_shift": bell_draw(arg_keys[3], (CH,), 0.5, 3.0, (), jnp.float32),
        "w_spatial": bell_draw(arg_keys[4], (3, 3, CH, CH), (9 * CH) ** -0.5, 0.125),
        "b_spatial": bell_draw(arg_keys[5], (CH,), 0.5, 3.0, (), jnp.float32),
        "w_time": bell_draw(arg_keys[6], (3, CH, CH), (2 * CH) ** -0.5, 0.25),
        "b_time": bell_draw(arg_keys[7], (CH,), 0.5, 3.0, (), jnp.float32),
        "w_lift": bell_draw(arg_keys[8], (CH, CH_OUT), CH ** -0.5, 0.375),
        "pack_dest": draw_pack_dest(jax.random.fold_in(arg_keys[10], 71), 0),
    }


HIGH = lax.Precision.HIGHEST

def reference(frames, clip_ids, norm_gain, norm_shift, w_spatial, b_spatial, w_time, b_time, w_lift, pack_dest):
    nfr, hgt, wid, chan = frames.shape
    per_group = chan // GROUPS
    onehot = (clip_ids[:, None] == jnp.arange(CLIPS, dtype=jnp.int32)[None, :]).astype(jnp.float32)

    def frame_stats(frame):
        grouped = frame.astype(jnp.float32).reshape(hgt * wid, GROUPS, per_group)
        return (lax.optimization_barrier(jnp.sum(grouped, axis=(0, 2))), lax.optimization_barrier(jnp.sum(grouped * grouped, axis=(0, 2))))
    sums, squares = lax.map(frame_stats, frames)
    counts = lax.optimization_barrier(jnp.sum(onehot, axis=0)) * (hgt * wid * per_group)
    clip_sum = jnp.dot(onehot.T, sums, precision=HIGH)
    clip_sq = jnp.dot(onehot.T, squares, precision=HIGH)
    mean = clip_sum / counts[:, None]
    var = clip_sq / counts[:, None] - mean * mean
    rstd = 1.0 / jnp.sqrt(var + 1e-05)
    frame_mean = jnp.dot(onehot, mean, precision=HIGH)
    frame_rstd = jnp.dot(onehot, rstd, precision=HIGH)
    wsp = w_spatial.astype(jnp.float32)
    wtm = w_time.astype(jnp.float32)

    def spatial_frame(args):
        frame, fmean, frstd = args
        grouped = frame.astype(jnp.float32).reshape(hgt, wid, GROUPS, per_group)
        normed = ((grouped - fmean[None, None, :, None]) * frstd[None, None, :, None]).reshape(hgt, wid, chan)
        normed = jax.nn.silu(normed * norm_gain + norm_shift).astype(jnp.bfloat16).astype(jnp.float32)
        padded = jnp.pad(normed, ((1, 1), (1, 1), (0, 0)))
        total = jnp.zeros((hgt, wid, chan), jnp.float32) + b_spatial
        for a in range(3):
            for b in range(3):
                total = total + jnp.einsum('hwc,cd->hwd', padded[a:a + hgt, b:b + wid], wsp[a, b], precision=HIGH)
        return total.astype(jnp.bfloat16)
    spatial = lax.map(spatial_frame, (frames, frame_mean, frame_rstd))
    spatial_pad = jnp.concatenate([jnp.zeros((2, hgt, wid, chan), jnp.bfloat16), spatial], axis=0)
    ids_pad = jnp.concatenate([jnp.full((2,), -1, jnp.int32), clip_ids])
    wlf = w_lift.astype(jnp.float32)

    def time_frame(index):
        total = frames[index].astype(jnp.float32) + b_time
        for k in range(3):
            source = lax.dynamic_index_in_dim(spatial_pad, index + 2 - k, 0, keepdims=False).astype(jnp.float32)
            same = (lax.dynamic_index_in_dim(ids_pad, index + 2 - k, 0, keepdims=False) == clip_ids[index]).astype(jnp.float32)
            total = total + same * jnp.einsum('hwc,cd->hwd', source, wtm[k], precision=HIGH)
        lifted_in = total.astype(jnp.bfloat16).astype(jnp.float32)
        return jnp.einsum('hwc,cd->hwd', lifted_in, wlf, precision=HIGH).astype(jnp.bfloat16)
    lifted = lax.map(time_frame, jnp.arange(nfr, dtype=jnp.int32))
    packed = jnp.zeros_like(lifted).at[pack_dest].set(lifted)
    return packed
```

```python
import functools

import jax
import jax.numpy as jnp
from jax import lax
from jax.experimental import pallas as pl
from jax.experimental.pallas import tpu as pltpu
from jax.sharding import PartitionSpec as P

GROUPS = 32
CLIPS = 16
BACK = 2
LEAD = 8
DIRECT = 4
MESH = pl.DeviceIdType.MESH
HIGH = lax.Precision.HIGHEST
F32 = jnp.float32
BF16 = jnp.bfloat16


def flipped(index, mask, count):
    out, bit = 0, 1
    while bit < count:
        out = out + lax.rem(lax.rem(index // bit, 2) + lax.rem(mask // bit, 2), 2) * bit
        bit *= 2
    return out


def block_kernel(
    shards,
    bands,
    width,
    order_ref,
    frames_ref,
    ids_ref,
    pos_ref,
    gain_ref,
    shift_ref,
    wsp_ref,
    bsp_ref,
    wtm_ref,
    btm_ref,
    got_ref,
    gotpos_ref,
    xin,
    idtab,
    mean_t,
    scale_t,
    nbuf,
    spat,
    sendbuf,
    rbuf,
    sbuf,
    load_sem,
    halo_send,
    halo_recv,
    r_send,
    r_recv,
    s_send,
    s_recv,
    p_send,
    p_recv,
    x_send,
    x_recv,
    own_sem,
):
    count, cells, chan = frames_ref.shape
    per_peer = count // shards
    per_group = chan // GROUPS
    band = cells // width
    me = lax.axis_index("slab")
    row = lax.axis_index("rows")
    direct = min(DIRECT, (shards - 1) * per_peer)

    def load(t):
        return pltpu.make_async_copy(
            frames_ref.at[t], xin.at[t + BACK, pl.ds(width, cells)], load_sem.at[t]
        )

    @pl.loop(0, count)
    def _(t):
        load(t).start()

    barrier = pltpu.get_barrier_semaphore()
    for o in range(1, bands):
        pl.semaphore_signal(
            barrier, inc=1, device_id=(me, lax.rem(row + o, bands)), device_id_type=MESH
        )
    for o in range(1, shards):
        pl.semaphore_signal(
            barrier, inc=1, device_id=(lax.rem(me + o, shards), row), device_id_type=MESH
        )
    for a in (1, shards - 1):
        for b in (1, bands - 1):
            pl.semaphore_signal(
                barrier,
                inc=1,
                device_id=(lax.rem(me + a, shards), lax.rem(row + b, bands)),
                device_id_type=MESH,
            )
    pl.semaphore_wait(barrier, bands - 1 + shards - 1 + 4)

    top = pl.ds(0, width)
    bottom = pl.ds(width + cells, width)
    first = pl.ds(0, width)
    last = pl.ds(cells - width, width)
    own = pl.ds(BACK, count)
    tail = pl.ds(count - BACK, BACK)
    prior = pl.ds(0, BACK)
    up_slab = lax.rem(me + 1, shards)
    up_row = lax.rem(row + 1, bands)
    down_row = lax.rem(row + bands - 1, bands)

    def halo(i, src, dst, slab, band_index):
        return pltpu.make_async_remote_copy(
            src_ref=src,
            dst_ref=dst,
            send_sem=halo_send.at[i],
            recv_sem=halo_recv.at[i],
            device_id=(slab, band_index),
            device_id_type=MESH,
        )

    halos = (
        (
            halo(0, frames_ref.at[tail], xin.at[prior, pl.ds(width, cells)], up_slab, row),
            me < shards - 1,
            me > 0,
        ),
        (
            halo(1, frames_ref.at[tail, last], xin.at[prior, top], up_slab, up_row),
            jnp.logical_and(me < shards - 1, row < bands - 1),
            jnp.logical_and(me > 0, row > 0),
        ),
        (
            halo(2, frames_ref.at[tail, first], xin.at[prior, bottom], up_slab, down_row),
            jnp.logical_and(me < shards - 1, row > 0),
            jnp.logical_and(me > 0, row < bands - 1),
        ),
        (
            halo(3, frames_ref.at[:, last], xin.at[own, top], me, up_row),
            row < bands - 1,
            row > 0,
        ),
        (
            halo(4, frames_ref.at[:, first], xin.at[own, bottom], me, down_row),
            row > 0,
            row < bands - 1,
        ),
        (
            halo(5, ids_ref.at[pl.ds(count - LEAD, LEAD)], idtab.at[pl.ds(0, LEAD)], up_slab, row),
            me < shards - 1,
            me > 0,
        ),
    )
    for copy, sends, _ in halos:

        @pl.when(sends)
        def _(copy=copy):
            copy.start()

    def place(d):
        return pltpu.make_async_remote_copy(
            src_ref=pos_ref.at[d],
            dst_ref=gotpos_ref.at[me],
            send_sem=p_send.at[d],
            recv_sem=p_recv.at[me],
            device_id=(d, row),
            device_id_type=MESH,
        )

    idtab[pl.ds(LEAD, count), :] = ids_ref[...]
    clip_row = lax.broadcasted_iota(jnp.int32, (CLIPS, chan), 0)
    zero = jnp.zeros((CLIPS, chan), F32)

    def stats(t, carry):
        total, squares, number = carry
        load(t).wait()
        x = xin[t + BACK, pl.ds(width, cells), :].astype(F32)
        one = jnp.sum(x, axis=0, keepdims=True)
        two = jnp.sum(x * x, axis=0, keepdims=True)
        mine = clip_row == ids_ref[pl.ds(t, 1), :]
        return (
            total + jnp.where(mine, one, 0.0),
            squares + jnp.where(mine, two, 0.0),
            number + jnp.where(mine, 1.0, 0.0),
        )

    total, squares, number = lax.fori_loop(0, count, stats, (zero, zero, zero))
    lanes = 128
    channel = lax.broadcasted_iota(jnp.int32, (chan, lanes), 0)
    lane = lax.broadcasted_iota(jnp.int32, (chan, lanes), 1)

    def member(channel, lane, start):
        low = (lane - start) * per_group
        return jnp.logical_and(channel >= low, channel < low + per_group).astype(F32)

    table = jnp.dot(
        total, member(channel, lane, 0), precision=HIGH, preferred_element_type=F32
    ) + jnp.dot(
        squares, member(channel, lane, GROUPS), precision=HIGH, preferred_element_type=F32
    )
    lane_c = lax.broadcasted_iota(jnp.int32, (CLIPS, lanes), 1)
    table = jnp.where(lane_c == 2 * GROUPS, number[:, :lanes] * float(cells * per_group), table)

    rbuf[row] = table

    def across_rows(peer, src):
        return pltpu.make_async_remote_copy(
            src_ref=rbuf.at[src],
            dst_ref=rbuf.at[src],
            send_sem=r_send.at[peer],
            recv_sem=r_recv.at[src],
            device_id=(me, peer),
            device_id_type=MESH,
        )

    for o in range(1, bands):
        across_rows(lax.rem(row + o, bands), row).start()
    for o in range(1, bands):
        peer = lax.rem(row + o, bands)
        across_rows(peer, peer).wait_recv()
    part = rbuf[0]
    for i in range(1, bands):
        part = part + rbuf[i]
    sbuf[me] = part

    def across_slab(peer, src):
        return pltpu.make_async_remote_copy(
            src_ref=sbuf.at[src],
            dst_ref=sbuf.at[src],
            send_sem=s_send.at[peer],
            recv_sem=s_recv.at[src],
            device_id=(peer, row),
            device_id_type=MESH,
        )

    for o in range(1, shards):
        across_slab(lax.rem(me + o, shards), me).start()
    for o in range(1, shards):
        place(lax.rem(me + o, shards)).start()
    for o in range(1, shards):
        peer = lax.rem(me + o, shards)
        across_slab(peer, peer).wait_recv()
    whole = sbuf[0]
    for i in range(1, shards):
        whole = whole + sbuf[i]

    lane_e = lax.broadcasted_iota(jnp.int32, (lanes, chan), 0)
    channel_e = lax.broadcasted_iota(jnp.int32, (lanes, chan), 1)

    def spread(matrix):
        return jnp.dot(whole, matrix, precision=HIGH, preferred_element_type=F32)

    cnt = spread((lane_e == 2 * GROUPS).astype(F32))
    mean = spread(member(channel_e, lane_e, 0)) / cnt
    var = spread(member(channel_e, lane_e, GROUPS)) / cnt - mean * mean
    scale = gain_ref[...] * (1.0 / jnp.sqrt(var + 1e-05))

    for copy, _, receives in halos:

        @pl.when(receives)
        def _(copy=copy):
            copy.wait_recv()

    @pl.when(me == 0)
    def _():
        idtab[pl.ds(0, LEAD), :] = jnp.full((LEAD, chan), -1, jnp.int32)

    ids = idtab[...]
    frame_mean = jnp.zeros(ids.shape, F32)
    frame_scale = jnp.zeros(ids.shape, F32)
    for c in range(CLIPS):
        frame_mean = jnp.where(ids == c, mean[c : c + 1, :], frame_mean)
        frame_scale = jnp.where(ids == c, scale[c : c + 1, :], frame_scale)
    mean_t[...] = frame_mean
    scale_t[...] = frame_scale

    shift = shift_ref[...]
    bsp = bsp_ref[...]
    btm = btm_ref[...]
    column = lax.broadcasted_iota(jnp.int32, (width, chan), 0)

    def spatial_frame(f, e):
        mu = mean_t[pl.ds(f + LEAD - BACK, 1), :]
        sc = scale_t[pl.ds(f + LEAD - BACK, 1), :]
        for i in range(band + 2):
            x = xin[f, pl.ds(i * width, width), :].astype(F32)
            v = (x - mu) * sc + shift
            half = 0.5 * v
            y = half + half * jnp.tanh(half)
            if i == 0:
                y = jnp.where(row > 0, y, 0.0)
            if i == band + 1:
                y = jnp.where(row < bands - 1, y, 0.0)
            rows_i = pl.ds(i * width, width)
            left = jnp.where(column == 0, 0.0, pltpu.roll(y, 1, 0))
            right = jnp.where(column == width - 1, 0.0, pltpu.roll(y, width - 1, 0))
            nbuf[rows_i, pl.ds(0, chan)] = left.astype(BF16)
            nbuf[rows_i, pl.ds(chan, chan)] = y.astype(BF16)
            nbuf[rows_i, pl.ds(2 * chan, chan)] = right.astype(BF16)
        for m in range(0, cells, 2 * width):
            size = min(2 * width, cells - m)
            acc = jnp.dot(nbuf[pl.ds(m, size), :], wsp_ref[0], preferred_element_type=F32)
            for a in (1, 2):
                acc = acc + jnp.dot(
                    nbuf[pl.ds(m + a * width, size), :], wsp_ref[a], preferred_element_type=F32
                )
            spat[e, pl.ds(m, size), :] = (acc + bsp).astype(BF16)

    def slot_frame(slot, entry):
        t = order_ref[slot]
        now = idtab[pl.ds(t + LEAD, 1), :]
        for m in range(0, cells, 2 * width):
            size = min(2 * width, cells - m)
            acc = xin[t + BACK, pl.ds(width + m, size), :].astype(F32) + btm
            for k in range(BACK + 1):
                term = jnp.dot(
                    spat[entry(t, k), pl.ds(m, size), :], wtm_ref[k], preferred_element_type=F32
                )
                if k > 0:
                    same = idtab[pl.ds(t + LEAD - k, 1), :] == now
                    term = jnp.where(same, term, 0.0)
                acc = acc + term
            sendbuf[slot, pl.ds(m, size), :] = acc.astype(BF16)

    def exchange(d, src, q):
        return pltpu.make_async_remote_copy(
            src_ref=sendbuf.at[d * per_peer + q],
            dst_ref=got_ref.at[src * per_peer + q],
            send_sem=x_send.at[d * per_peer + q],
            recv_sem=x_recv.at[src * per_peer + q],
            device_id=(d, row),
            device_id_type=MESH,
        )

    def target(i):
        return flipped(me, shards - 1 - i // per_peer, shards), lax.rem(i, per_peer)

    @pl.loop(0, direct)
    def _(i):
        d, q = target(i)
        slot = d * per_peer + q

        @pl.loop(0, BACK + 1)
        def _(k):
            spatial_frame(order_ref[slot] + BACK - k, count + BACK + k)

        slot_frame(slot, lambda t, k: count + BACK + k)
        exchange(d, me, q).start()

    @pl.loop(0, count + BACK)
    def _(f):
        spatial_frame(f, f)

    @pl.loop(direct, (shards - 1) * per_peer)
    def _(i):
        d, q = target(i)
        slot_frame(d * per_peer + q, lambda t, k: t + BACK - k)
        exchange(d, me, q).start()

    def keep(q):
        return pltpu.make_async_copy(
            sendbuf.at[me * per_peer + q], got_ref.at[me * per_peer + q], own_sem.at[q]
        )

    keep_pos = pltpu.make_async_copy(pos_ref.at[me], gotpos_ref.at[me], own_sem.at[per_peer])
    keep_pos.start()
    for q in range(per_peer):
        slot_frame(me * per_peer + q, lambda t, k: t + BACK - k)
        keep(q).start()

    for copy, sends, _ in halos:

        @pl.when(sends)
        def _(copy=copy):
            copy.wait_send()

    for o in range(1, bands):
        across_rows(lax.rem(row + o, bands), row).wait_send()
    for o in range(1, shards):
        across_slab(lax.rem(me + o, shards), me).wait_send()
    for o in range(1, shards):
        peer = lax.rem(me + o, shards)
        place(peer).wait_send()
        pltpu.make_async_remote_copy(
            src_ref=pos_ref.at[peer],
            dst_ref=gotpos_ref.at[peer],
            send_sem=p_send.at[peer],
            recv_sem=p_recv.at[peer],
            device_id=(peer, row),
            device_id_type=MESH,
        ).wait_recv()
    keep_pos.wait()
    for q in range(per_peer):
        keep(q).wait()

    @pl.loop(0, (shards - 1) * per_peer)
    def _(i):
        d, q = target(i)
        exchange(d, me, q).wait_send()
        exchange(d, d, q).wait_recv()


def lift_kernel(pos_ref, x_ref, w_ref, o_ref):
    del pos_ref
    o_ref[0] = jnp.dot(x_ref[0], w_ref[...], preferred_element_type=F32).astype(BF16)


def route(pack_dest, shards):
    count = pack_dest.shape[0]
    per_peer = count // shards
    target = pack_dest // count
    index = jnp.arange(count, dtype=jnp.int32)
    earlier = jnp.logical_and(target[:, None] == target[None, :], index[:, None] < index[None, :])
    slot_of = target * per_peer + jnp.sum(earlier.astype(jnp.int32), axis=0)
    selector = (slot_of[None, :] == index[:, None]).astype(jnp.int32)
    order = jnp.sum(selector * index[None, :], axis=1)
    position = jnp.sum(selector * (pack_dest % count)[None, :], axis=1)
    return order, position


def body(
    frames, clip_ids, norm_gain, norm_shift, w_spatial, b_spatial, w_time, b_time, w_lift, pack_dest
):
    count, band, width, chan = frames.shape
    lifted = w_lift.shape[1]
    cells = band * width
    shards = lax.axis_size("slab")
    bands = lax.axis_size("rows")
    per_peer = count // shards
    order, position = route(pack_dest, shards)
    pos = jnp.pad(position.reshape(shards, 1, per_peer), ((0, 0), (0, 0), (0, 128 - per_peer)))
    pos = jnp.broadcast_to(pos, (shards, 8, 128))
    ids = jnp.broadcast_to(clip_ids[:, None], (count, chan))
    vmem = pl.BlockSpec(memory_space=pltpu.VMEM)
    hbm = pl.BlockSpec(memory_space=pl.ANY)
    dma = pltpu.SemaphoreType.DMA
    got, gotpos = pl.pallas_call(
        functools.partial(block_kernel, shards, bands, width),
        out_shape=(
            jax.ShapeDtypeStruct((count, cells, chan), BF16),
            jax.ShapeDtypeStruct((shards, 8, 128), jnp.int32),
        ),
        in_specs=[pl.BlockSpec(memory_space=pltpu.SMEM), hbm] + [vmem] * 8,
        out_specs=(hbm, hbm),
        scratch_shapes=[
            pltpu.VMEM((count + BACK, cells + 2 * width, chan), BF16),
            pltpu.VMEM((LEAD + count, chan), jnp.int32),
            pltpu.VMEM((LEAD + count, chan), F32),
            pltpu.VMEM((LEAD + count, chan), F32),
            pltpu.VMEM((cells + 2 * width, 3 * chan), BF16),
            pltpu.VMEM((count + 2 * BACK + 1, cells, chan), BF16),
            pltpu.VMEM((count, cells, chan), BF16),
            pltpu.VMEM((bands, CLIPS, 128), F32),
            pltpu.VMEM((shards, CLIPS, 128), F32),
            dma((count,)),
            dma((6,)),
            dma((6,)),
            dma((bands,)),
            dma((bands,)),
            dma((shards,)),
            dma((shards,)),
            dma((shards,)),
            dma((shards,)),
            dma((count,)),
            dma((count,)),
            dma((per_peer + 1,)),
        ],
        compiler_params=pltpu.CompilerParams(
            collective_id=0, has_side_effects=True, vmem_limit_bytes=44 * 1024 * 1024
        ),
        name="block",
    )(
        order,
        frames.reshape(count, cells, chan),
        ids,
        pos,
        norm_gain.reshape(1, chan),
        norm_shift.reshape(1, chan),
        w_spatial.reshape(3, 3 * chan, chan),
        b_spatial.reshape(1, chan),
        w_time,
        b_time.reshape(1, chan),
    )
    where_to = gotpos[:, 0, :per_peer].reshape(count)
    packed = pl.pallas_call(
        lift_kernel,
        out_shape=jax.ShapeDtypeStruct((count, cells, lifted), BF16),
        grid_spec=pltpu.PrefetchScalarGridSpec(
            num_scalar_prefetch=1,
            grid=(count,),
            in_specs=[
                pl.BlockSpec((1, cells, chan), lambda s, p: (s, 0, 0)),
                pl.BlockSpec((chan, lifted), lambda s, p: (0, 0)),
            ],
            out_specs=pl.BlockSpec((1, cells, lifted), lambda s, p: (p[s], 0, 0)),
        ),
        compiler_params=pltpu.CompilerParams(vmem_limit_bytes=16 * 1024 * 1024),
        name="lift",
    )(where_to, got, w_lift)
    return packed.reshape(count, band, width, lifted)


def solution(mesh):
    in_specs = (
        P("slab", "rows", None, None),
        P("slab"),
        P(),
        P(),
        P(),
        P(),
        P(),
        P(),
        P(),
        P("slab"),
    )
    out_specs = P("slab", "rows", None, None)
    return jax.shard_map(body, mesh=mesh, in_specs=in_specs, out_specs=out_specs, check_vma=False)
```

```python
import functools

import jax
import jax.numpy as jnp
from jax import lax
from jax.experimental import pallas as pl
from jax.experimental.pallas import tpu as pltpu
from jax.sharding import PartitionSpec as P

GROUPS = 32
CLIPS = 16
BACK = 2
LEAD = 8
DIRECT = 5
MESH = pl.DeviceIdType.MESH
HIGH = lax.Precision.HIGHEST
F32 = jnp.float32
BF16 = jnp.bfloat16


def flipped(index, mask, count):
    out, bit = 0, 1
    while bit < count:
        out = out + lax.rem(lax.rem(index // bit, 2) + lax.rem(mask // bit, 2), 2) * bit
        bit *= 2
    return out


def block_kernel(
    shards,
    bands,
    width,
    order_ref,
    frames_ref,
    ids_ref,
    pos_ref,
    gain_hbm,
    shift_hbm,
    bsp_hbm,
    btm_hbm,
    wsp_hbm,
    wtm_hbm,
    got_ref,
    gotpos_ref,
    xin,
    idtab,
    mean_t,
    scale_t,
    nbuf,
    spat,
    sendbuf,
    rbuf,
    sbuf,
    rows_v,
    wsp_ref,
    wtm_ref,
    load_sem,
    param_sem,
    halo_send,
    halo_recv,
    r_send,
    r_recv,
    s_send,
    s_recv,
    p_send,
    p_recv,
    x_send,
    x_recv,
    own_sem,
):
    count, cells, chan = frames_ref.shape
    per_peer = count // shards
    per_group = chan // GROUPS
    band = cells // width
    me = lax.axis_index("slab")
    row = lax.axis_index("rows")
    group = BACK + 1
    direct = min(DIRECT, (shards - 1) * per_peer)

    def load(t):
        return pltpu.make_async_copy(
            frames_ref.at[t], xin.at[t + BACK, pl.ds(width, cells)], load_sem.at[t]
        )

    @pl.loop(0, count)
    def _(t):
        load(t).start()

    params = [
        pltpu.make_async_copy(src, dst, param_sem.at[i])
        for i, (src, dst) in enumerate(
            (
                (gain_hbm, rows_v.at[0]),
                (shift_hbm, rows_v.at[1]),
                (bsp_hbm, rows_v.at[2]),
                (btm_hbm, rows_v.at[3]),
                (wsp_hbm, wsp_ref),
                (wtm_hbm, wtm_ref),
            )
        )
    ]
    for copy in params:
        copy.start()

    barrier = pltpu.get_barrier_semaphore()
    for o in range(1, bands):
        pl.semaphore_signal(
            barrier, inc=1, device_id=(me, lax.rem(row + o, bands)), device_id_type=MESH
        )
    for o in range(1, shards):
        pl.semaphore_signal(
            barrier, inc=1, device_id=(lax.rem(me + o, shards), row), device_id_type=MESH
        )
    for a in (1, shards - 1):
        for b in (1, bands - 1):
            pl.semaphore_signal(
                barrier,
                inc=1,
                device_id=(lax.rem(me + a, shards), lax.rem(row + b, bands)),
                device_id_type=MESH,
            )
    pl.semaphore_wait(barrier, bands - 1 + shards - 1 + 4)

    top = pl.ds(0, width)
    bottom = pl.ds(width + cells, width)
    first = pl.ds(0, width)
    last = pl.ds(cells - width, width)
    own = pl.ds(BACK, count)
    tail = pl.ds(count - BACK, BACK)
    prior = pl.ds(0, BACK)
    up_slab = lax.rem(me + 1, shards)
    up_row = lax.rem(row + 1, bands)
    down_row = lax.rem(row + bands - 1, bands)

    def halo(i, src, dst, slab, band_index):
        return pltpu.make_async_remote_copy(
            src_ref=src,
            dst_ref=dst,
            send_sem=halo_send.at[i],
            recv_sem=halo_recv.at[i],
            device_id=(slab, band_index),
            device_id_type=MESH,
        )

    halos = (
        (
            halo(0, frames_ref.at[tail], xin.at[prior, pl.ds(width, cells)], up_slab, row),
            me < shards - 1,
            me > 0,
        ),
        (
            halo(1, frames_ref.at[tail, last], xin.at[prior, top], up_slab, up_row),
            jnp.logical_and(me < shards - 1, row < bands - 1),
            jnp.logical_and(me > 0, row > 0),
        ),
        (
            halo(2, frames_ref.at[tail, first], xin.at[prior, bottom], up_slab, down_row),
            jnp.logical_and(me < shards - 1, row > 0),
            jnp.logical_and(me > 0, row < bands - 1),
        ),
        (
            halo(3, frames_ref.at[:, last], xin.at[own, top], me, up_row),
            row < bands - 1,
            row > 0,
        ),
        (
            halo(4, frames_ref.at[:, first], xin.at[own, bottom], me, down_row),
            row > 0,
            row < bands - 1,
        ),
        (
            halo(5, ids_ref.at[pl.ds(count - LEAD, LEAD)], idtab.at[pl.ds(0, LEAD)], up_slab, row),
            me < shards - 1,
            me > 0,
        ),
    )
    for copy, sends, _ in halos:

        @pl.when(sends)
        def _(copy=copy):
            copy.start()

    def place(d):
        return pltpu.make_async_remote_copy(
            src_ref=pos_ref.at[d],
            dst_ref=gotpos_ref.at[me],
            send_sem=p_send.at[d],
            recv_sem=p_recv.at[me],
            device_id=(d, row),
            device_id_type=MESH,
        )

    idtab[pl.ds(LEAD, count), :] = ids_ref[...]
    clip_row = lax.broadcasted_iota(jnp.int32, (CLIPS, chan), 0)
    zero = jnp.zeros((CLIPS, chan), F32)

    def stats(t, carry):
        total, squares, number = carry
        load(t).wait()
        x = xin[t + BACK, pl.ds(width, cells), :].astype(F32)
        one = jnp.sum(x, axis=0, keepdims=True)
        two = jnp.sum(x * x, axis=0, keepdims=True)
        mine = clip_row == ids_ref[pl.ds(t, 1), :]
        return (
            total + jnp.where(mine, one, 0.0),
            squares + jnp.where(mine, two, 0.0),
            number + jnp.where(mine, 1.0, 0.0),
        )

    total, squares, number = lax.fori_loop(0, count, stats, (zero, zero, zero))
    lanes = 128
    channel = lax.broadcasted_iota(jnp.int32, (chan, lanes), 0)
    lane = lax.broadcasted_iota(jnp.int32, (chan, lanes), 1)

    def member(channel, lane, start):
        low = (lane - start) * per_group
        return jnp.logical_and(channel >= low, channel < low + per_group).astype(F32)

    table = jnp.dot(
        total, member(channel, lane, 0), precision=HIGH, preferred_element_type=F32
    ) + jnp.dot(
        squares, member(channel, lane, GROUPS), precision=HIGH, preferred_element_type=F32
    )
    lane_c = lax.broadcasted_iota(jnp.int32, (CLIPS, lanes), 1)
    table = jnp.where(lane_c == 2 * GROUPS, number[:, :lanes] * float(cells * per_group), table)

    rbuf[row] = table

    def across_rows(peer, src):
        return pltpu.make_async_remote_copy(
            src_ref=rbuf.at[src],
            dst_ref=rbuf.at[src],
            send_sem=r_send.at[peer],
            recv_sem=r_recv.at[src],
            device_id=(me, peer),
            device_id_type=MESH,
        )

    for o in range(1, bands):
        across_rows(lax.rem(row + o, bands), row).start()
    for o in range(1, bands):
        peer = lax.rem(row + o, bands)
        across_rows(peer, peer).wait_recv()
    part = rbuf[0]
    for i in range(1, bands):
        part = part + rbuf[i]
    sbuf[me] = part

    def across_slab(peer, src):
        return pltpu.make_async_remote_copy(
            src_ref=sbuf.at[src],
            dst_ref=sbuf.at[src],
            send_sem=s_send.at[peer],
            recv_sem=s_recv.at[src],
            device_id=(peer, row),
            device_id_type=MESH,
        )

    for o in range(1, shards):
        across_slab(lax.rem(me + o, shards), me).start()
    for o in range(1, shards):
        place(lax.rem(me + o, shards)).start()
    for o in range(1, shards):
        peer = lax.rem(me + o, shards)
        across_slab(peer, peer).wait_recv()
    whole = sbuf[0]
    for i in range(1, shards):
        whole = whole + sbuf[i]

    lane_e = lax.broadcasted_iota(jnp.int32, (lanes, chan), 0)
    channel_e = lax.broadcasted_iota(jnp.int32, (lanes, chan), 1)

    def spread(matrix):
        return jnp.dot(whole, matrix, precision=HIGH, preferred_element_type=F32)

    for copy in params:
        copy.wait()
    cnt = spread((lane_e == 2 * GROUPS).astype(F32))
    mean = spread(member(channel_e, lane_e, 0)) / cnt
    var = spread(member(channel_e, lane_e, GROUPS)) / cnt - mean * mean
    scale = rows_v[0] * (1.0 / jnp.sqrt(var + 1e-05))

    for copy, _, receives in halos:

        @pl.when(receives)
        def _(copy=copy):
            copy.wait_recv()

    @pl.when(me == 0)
    def _():
        idtab[pl.ds(0, LEAD), :] = jnp.full((LEAD, chan), -1, jnp.int32)

    ids = idtab[...]
    frame_mean = jnp.zeros(ids.shape, F32)
    frame_scale = jnp.zeros(ids.shape, F32)
    for c in range(CLIPS):
        frame_mean = jnp.where(ids == c, mean[c : c + 1, :], frame_mean)
        frame_scale = jnp.where(ids == c, scale[c : c + 1, :], frame_scale)
    mean_t[...] = frame_mean
    scale_t[...] = frame_scale

    shift = rows_v[1]
    bsp = rows_v[2]
    btm = rows_v[3]
    column = lax.broadcasted_iota(jnp.int32, (width, chan), 0)

    def normalise(f, place_at):
        mu = mean_t[pl.ds(f + LEAD - BACK, 1), :]
        sc = scale_t[pl.ds(f + LEAD - BACK, 1), :]
        for i in range(band + 2):
            x = xin[f, pl.ds(i * width, width), :].astype(F32)
            v = (x - mu) * sc + shift
            half = 0.5 * v
            y = half + half * jnp.tanh(half)
            if i == 0:
                y = jnp.where(row > 0, y, 0.0)
            if i == band + 1:
                y = jnp.where(row < bands - 1, y, 0.0)
            left = jnp.where(column == 0, 0.0, pltpu.roll(y, 1, 0))
            right = jnp.where(column == width - 1, 0.0, pltpu.roll(y, width - 1, 0))
            nbuf[i, place_at, :, pl.ds(0, chan)] = left.astype(BF16)
            nbuf[i, place_at, :, pl.ds(chan, chan)] = y.astype(BF16)
            nbuf[i, place_at, :, pl.ds(2 * chan, chan)] = right.astype(BF16)

    def convolve(entry):
        size = band * group * width
        acc = jnp.zeros((size, chan), F32) + bsp
        for a in range(3):
            acc = acc + jnp.dot(
                nbuf[pl.ds(a, band)].reshape(size, 3 * chan),
                wsp_ref[a],
                preferred_element_type=F32,
            )
        out = acc.astype(BF16).reshape(band, group, width, chan)
        for i in range(band):
            for g in range(group):
                spat[entry + g, pl.ds(i * width, width), :] = out[i, g]

    def slot_frame(slot, entry):
        t = order_ref[slot]
        now = idtab[pl.ds(t + LEAD, 1), :]
        acc = xin[t + BACK, pl.ds(width, cells), :].astype(F32) + btm
        for k in range(BACK + 1):
            term = jnp.dot(spat[entry(t, k)], wtm_ref[k], preferred_element_type=F32)
            if k > 0:
                same = idtab[pl.ds(t + LEAD - k, 1), :] == now
                term = jnp.where(same, term, 0.0)
            acc = acc + term
        sendbuf[slot] = acc.astype(BF16)

    def exchange(d, src, q):
        return pltpu.make_async_remote_copy(
            src_ref=sendbuf.at[d * per_peer + q],
            dst_ref=got_ref.at[src * per_peer + q],
            send_sem=x_send.at[d * per_peer + q],
            recv_sem=x_recv.at[src * per_peer + q],
            device_id=(d, row),
            device_id_type=MESH,
        )

    def target(i):
        return flipped(me, shards - 1 - i // per_peer, shards), lax.rem(i, per_peer)

    @pl.loop(0, direct)
    def _(i):
        d, q = target(i)
        slot = d * per_peer + q

        @pl.loop(0, BACK + 1)
        def _(k):
            normalise(order_ref[slot] + BACK - k, k)

        convolve(count + BACK)

        slot_frame(slot, lambda t, k: count + BACK + k)
        exchange(d, me, q).start()

    @pl.loop(0, (count + BACK) // group)
    def _(g):
        @pl.loop(0, group)
        def _(k):
            normalise(g * group + k, k)

        convolve(g * group)

    @pl.loop(direct, (shards - 1) * per_peer)
    def _(i):
        d, q = target(i)
        slot_frame(d * per_peer + q, lambda t, k: t + BACK - k)
        exchange(d, me, q).start()

    def keep(q):
        return pltpu.make_async_copy(
            sendbuf.at[me * per_peer + q], got_ref.at[me * per_peer + q], own_sem.at[q]
        )

    keep_pos = pltpu.make_async_copy(pos_ref.at[me], gotpos_ref.at[me], own_sem.at[per_peer])
    keep_pos.start()
    for q in range(per_peer):
        slot_frame(me * per_peer + q, lambda t, k: t + BACK - k)
        keep(q).start()

    for copy, sends, _ in halos:

        @pl.when(sends)
        def _(copy=copy):
            copy.wait_send()

    for o in range(1, bands):
        across_rows(lax.rem(row + o, bands), row).wait_send()
    for o in range(1, shards):
        across_slab(lax.rem(me + o, shards), me).wait_send()
    for o in range(1, shards):
        peer = lax.rem(me + o, shards)
        place(peer).wait_send()
        pltpu.make_async_remote_copy(
            src_ref=pos_ref.at[peer],
            dst_ref=gotpos_ref.at[peer],
            send_sem=p_send.at[peer],
            recv_sem=p_recv.at[peer],
            device_id=(peer, row),
            device_id_type=MESH,
        ).wait_recv()
    keep_pos.wait()
    for q in range(per_peer):
        keep(q).wait()

    @pl.loop(0, (shards - 1) * per_peer)
    def _(i):
        d, q = target(i)
        exchange(d, me, q).wait_send()
        exchange(d, d, q).wait_recv()


def lift_kernel(pos_ref, x_hbm, w_hbm, o_hbm, x, w, out, x_sem, w_sem, out_sem):
    count = x.shape[0]

    def load(s):
        return pltpu.make_async_copy(x_hbm.at[s], x.at[s], x_sem.at[s])

    def store(s):
        return pltpu.make_async_copy(out.at[s], o_hbm.at[pos_ref[s]], out_sem.at[s])

    weights = pltpu.make_async_copy(w_hbm, w, w_sem)
    weights.start()

    @pl.loop(0, count)
    def _(s):
        load(s).start()

    weights.wait()

    @pl.loop(0, count)
    def _(s):
        load(s).wait()
        out[s] = jnp.dot(x[s], w[...], preferred_element_type=F32).astype(BF16)
        store(s).start()

    @pl.loop(0, count)
    def _(s):
        store(s).wait()


def route(pack_dest, shards):
    count = pack_dest.shape[0]
    per_peer = count // shards
    target = pack_dest // count
    index = jnp.arange(count, dtype=jnp.int32)
    earlier = jnp.logical_and(target[:, None] == target[None, :], index[:, None] < index[None, :])
    slot_of = target * per_peer + jnp.sum(earlier.astype(jnp.int32), axis=0)
    selector = (slot_of[None, :] == index[:, None]).astype(jnp.int32)
    order = jnp.sum(selector * index[None, :], axis=1)
    position = jnp.sum(selector * (pack_dest % count)[None, :], axis=1)
    return order, position


def body(
    frames, clip_ids, norm_gain, norm_shift, w_spatial, b_spatial, w_time, b_time, w_lift, pack_dest
):
    count, band, width, chan = frames.shape
    lifted = w_lift.shape[1]
    cells = band * width
    shards = lax.axis_size("slab")
    bands = lax.axis_size("rows")
    per_peer = count // shards
    order, position = route(pack_dest, shards)
    pos = jnp.pad(position.reshape(shards, 1, per_peer), ((0, 0), (0, 0), (0, 128 - per_peer)))
    pos = jnp.broadcast_to(pos, (shards, 8, 128))
    ids = jnp.broadcast_to(clip_ids[:, None], (count, chan))
    vmem = pl.BlockSpec(memory_space=pltpu.VMEM)
    hbm = pl.BlockSpec(memory_space=pl.ANY)
    dma = pltpu.SemaphoreType.DMA
    got, gotpos = pl.pallas_call(
        functools.partial(block_kernel, shards, bands, width),
        out_shape=(
            jax.ShapeDtypeStruct((count, cells, chan), BF16),
            jax.ShapeDtypeStruct((shards, 8, 128), jnp.int32),
        ),
        in_specs=[pl.BlockSpec(memory_space=pltpu.SMEM), hbm, vmem, vmem] + [hbm] * 6,
        out_specs=(hbm, hbm),
        scratch_shapes=[
            pltpu.VMEM((count + BACK, cells + 2 * width, chan), BF16),
            pltpu.VMEM((LEAD + count, chan), jnp.int32),
            pltpu.VMEM((LEAD + count, chan), F32),
            pltpu.VMEM((LEAD + count, chan), F32),
            pltpu.VMEM((band + 2, BACK + 1, width, 3 * chan), BF16),
            pltpu.VMEM((count + 2 * BACK + 1, cells, chan), BF16),
            pltpu.VMEM((count, cells, chan), BF16),
            pltpu.VMEM((bands, CLIPS, 128), F32),
            pltpu.VMEM((shards, CLIPS, 128), F32),
            pltpu.VMEM((4, 1, chan), F32),
            pltpu.VMEM((3, 3 * chan, chan), BF16),
            pltpu.VMEM((BACK + 1, chan, chan), BF16),
            dma((count,)),
            dma((6,)),
            dma((6,)),
            dma((6,)),
            dma((bands,)),
            dma((bands,)),
            dma((shards,)),
            dma((shards,)),
            dma((shards,)),
            dma((shards,)),
            dma((count,)),
            dma((count,)),
            dma((per_peer + 1,)),
        ],
        compiler_params=pltpu.CompilerParams(
            collective_id=0, has_side_effects=True, vmem_limit_bytes=60 * 1024 * 1024
        ),
        name="block",
    )(
        order,
        frames.reshape(count, cells, chan),
        ids,
        pos,
        norm_gain.reshape(1, chan),
        norm_shift.reshape(1, chan),
        b_spatial.reshape(1, chan),
        b_time.reshape(1, chan),
        w_spatial.reshape(3, 3 * chan, chan),
        w_time,
    )
    where_to = gotpos[:, 0, :per_peer].reshape(count)
    packed = pl.pallas_call(
        lift_kernel,
        out_shape=jax.ShapeDtypeStruct((count, cells, lifted), BF16),
        in_specs=[pl.BlockSpec(memory_space=pltpu.SMEM), hbm, hbm],
        out_specs=hbm,
        scratch_shapes=[
            pltpu.VMEM((count, cells, chan), BF16),
            pltpu.VMEM((chan, lifted), BF16),
            pltpu.VMEM((count, cells, lifted), BF16),
            dma((count,)),
            dma,
            dma((count,)),
        ],
        compiler_params=pltpu.CompilerParams(vmem_limit_bytes=60 * 1024 * 1024),
        name="lift",
    )(where_to, got, w_lift)
    return packed.reshape(count, band, width, lifted)


def solution(mesh):
    in_specs = (
        P("slab", "rows", None, None),
        P("slab"),
        P(),
        P(),
        P(),
        P(),
        P(),
        P(),
        P(),
        P("slab"),
    )
    out_specs = P("slab", "rows", None, None)
    return jax.shard_map(body, mesh=mesh, in_specs=in_specs, out_specs=out_specs, check_vma=False)
```

```python
import functools

import jax
import jax.numpy as jnp
from jax import lax
from jax.experimental import pallas as pl
from jax.experimental.pallas import tpu as pltpu
from jax.sharding import PartitionSpec as P

GROUPS = 32
CLIPS = 16
BACK = 2
LEAD = 8
DIRECT = 6
MESH = pl.DeviceIdType.MESH
HIGH = lax.Precision.HIGHEST
F32 = jnp.float32
BF16 = jnp.bfloat16


def flipped(index, mask, count):
    out, bit = 0, 1
    while bit < count:
        out = out + lax.rem(lax.rem(index // bit, 2) + lax.rem(mask // bit, 2), 2) * bit
        bit *= 2
    return out


def block_kernel(
    shards,
    bands,
    width,
    order_ref,
    position_ref,
    clip_ref,
    frames_ref,
    gain_hbm,
    shift_hbm,
    bsp_hbm,
    btm_hbm,
    wsp_hbm,
    wtm_hbm,
    got_ref,
    gotpos_ref,
    xin,
    pos_ref,
    idtab,
    mean_t,
    scale_t,
    nbuf,
    spat,
    sendbuf,
    rbuf,
    sbuf,
    rows_v,
    wsp_ref,
    wtm_ref,
    load_sem,
    param_sem,
    halo_send,
    halo_recv,
    r_send,
    r_recv,
    s_send,
    s_recv,
    p_send,
    p_recv,
    x_send,
    x_recv,
    own_sem,
):
    count, cells, chan = frames_ref.shape
    per_peer = count // shards
    per_group = chan // GROUPS
    band = cells // width
    me = lax.axis_index("slab")
    row = lax.axis_index("rows")
    group = BACK + 1
    direct = min(DIRECT, (shards - 1) * per_peer)

    def load(t):
        return pltpu.make_async_copy(
            frames_ref.at[t], xin.at[t + BACK, pl.ds(width, cells)], load_sem.at[t]
        )

    @pl.loop(0, count)
    def _(t):
        load(t).start()

    params = [
        pltpu.make_async_copy(src, dst, param_sem.at[i])
        for i, (src, dst) in enumerate(
            (
                (gain_hbm, rows_v.at[0]),
                (shift_hbm, rows_v.at[1]),
                (bsp_hbm, rows_v.at[2]),
                (btm_hbm, rows_v.at[3]),
                (wsp_hbm, wsp_ref),
                (wtm_hbm, wtm_ref),
            )
        )
    ]
    for copy in params:
        copy.start()

    barrier = pltpu.get_barrier_semaphore()
    for o in range(1, bands):
        pl.semaphore_signal(
            barrier, inc=1, device_id=(me, lax.rem(row + o, bands)), device_id_type=MESH
        )
    for o in range(1, shards):
        pl.semaphore_signal(
            barrier, inc=1, device_id=(lax.rem(me + o, shards), row), device_id_type=MESH
        )
    for a in (1, shards - 1):
        for b in (1, bands - 1):
            pl.semaphore_signal(
                barrier,
                inc=1,
                device_id=(lax.rem(me + a, shards), lax.rem(row + b, bands)),
                device_id_type=MESH,
            )

    for t in range(count):
        idtab[LEAD + t : LEAD + t + 1, :] = jnp.full((1, chan), clip_ref[t], jnp.int32)
    pos_lane = lax.broadcasted_iota(jnp.int32, (1, 128), 1)
    for d in range(shards):
        line = jnp.zeros((1, 128), jnp.int32)
        for q in range(per_peer):
            line = jnp.where(pos_lane == q, position_ref[d * per_peer + q], line)
        pos_ref[d] = line
    pl.semaphore_wait(barrier, bands - 1 + shards - 1 + 4)

    top = pl.ds(0, width)
    bottom = pl.ds(width + cells, width)
    first = pl.ds(0, width)
    last = pl.ds(cells - width, width)
    own = pl.ds(BACK, count)
    tail = pl.ds(count - BACK, BACK)
    prior = pl.ds(0, BACK)
    up_slab = lax.rem(me + 1, shards)
    up_row = lax.rem(row + 1, bands)
    down_row = lax.rem(row + bands - 1, bands)

    def halo(i, src, dst, slab, band_index):
        return pltpu.make_async_remote_copy(
            src_ref=src,
            dst_ref=dst,
            send_sem=halo_send.at[i],
            recv_sem=halo_recv.at[i],
            device_id=(slab, band_index),
            device_id_type=MESH,
        )

    halos = (
        (
            halo(0, frames_ref.at[tail], xin.at[prior, pl.ds(width, cells)], up_slab, row),
            me < shards - 1,
            me > 0,
        ),
        (
            halo(1, frames_ref.at[tail, last], xin.at[prior, top], up_slab, up_row),
            jnp.logical_and(me < shards - 1, row < bands - 1),
            jnp.logical_and(me > 0, row > 0),
        ),
        (
            halo(2, frames_ref.at[tail, first], xin.at[prior, bottom], up_slab, down_row),
            jnp.logical_and(me < shards - 1, row > 0),
            jnp.logical_and(me > 0, row < bands - 1),
        ),
        (
            halo(3, frames_ref.at[:, last], xin.at[own, top], me, up_row),
            row < bands - 1,
            row > 0,
        ),
        (
            halo(4, frames_ref.at[:, first], xin.at[own, bottom], me, down_row),
            row > 0,
            row < bands - 1,
        ),
        (
            halo(5, idtab.at[pl.ds(count, LEAD)], idtab.at[pl.ds(0, LEAD)], up_slab, row),
            me < shards - 1,
            me > 0,
        ),
    )
    for copy, sends, _ in halos:

        @pl.when(sends)
        def _(copy=copy):
            copy.start()

    def place(d):
        return pltpu.make_async_remote_copy(
            src_ref=pos_ref.at[d],
            dst_ref=gotpos_ref.at[me],
            send_sem=p_send.at[d],
            recv_sem=p_recv.at[me],
            device_id=(d, row),
            device_id_type=MESH,
        )

    clip_row = lax.broadcasted_iota(jnp.int32, (CLIPS, chan), 0)
    zero = jnp.zeros((CLIPS, chan), F32)

    def stats(t, carry):
        total, squares, number = carry
        load(t).wait()
        x = xin[t + BACK, pl.ds(width, cells), :].astype(F32)
        one = jnp.sum(x, axis=0, keepdims=True)
        two = jnp.sum(x * x, axis=0, keepdims=True)
        mine = clip_row == idtab[pl.ds(t + LEAD, 1), :]
        return (
            total + jnp.where(mine, one, 0.0),
            squares + jnp.where(mine, two, 0.0),
            number + jnp.where(mine, 1.0, 0.0),
        )

    total, squares, number = lax.fori_loop(0, count, stats, (zero, zero, zero))
    lanes = 128
    channel = lax.broadcasted_iota(jnp.int32, (chan, lanes), 0)
    lane = lax.broadcasted_iota(jnp.int32, (chan, lanes), 1)

    def member(channel, lane, start):
        low = (lane - start) * per_group
        return jnp.logical_and(channel >= low, channel < low + per_group).astype(F32)

    table = jnp.dot(
        total, member(channel, lane, 0), precision=HIGH, preferred_element_type=F32
    ) + jnp.dot(
        squares, member(channel, lane, GROUPS), precision=HIGH, preferred_element_type=F32
    )
    lane_c = lax.broadcasted_iota(jnp.int32, (CLIPS, lanes), 1)
    table = jnp.where(lane_c == 2 * GROUPS, number[:, :lanes] * float(cells * per_group), table)

    rbuf[row] = table

    def across_rows(peer, src):
        return pltpu.make_async_remote_copy(
            src_ref=rbuf.at[src],
            dst_ref=rbuf.at[src],
            send_sem=r_send.at[peer],
            recv_sem=r_recv.at[src],
            device_id=(me, peer),
            device_id_type=MESH,
        )

    for o in range(1, bands):
        across_rows(lax.rem(row + o, bands), row).start()
    for o in range(1, bands):
        peer = lax.rem(row + o, bands)
        across_rows(peer, peer).wait_recv()
    part = rbuf[0]
    for i in range(1, bands):
        part = part + rbuf[i]
    sbuf[me] = part

    def across_slab(peer, src):
        return pltpu.make_async_remote_copy(
            src_ref=sbuf.at[src],
            dst_ref=sbuf.at[src],
            send_sem=s_send.at[peer],
            recv_sem=s_recv.at[src],
            device_id=(peer, row),
            device_id_type=MESH,
        )

    for o in range(1, shards):
        across_slab(lax.rem(me + o, shards), me).start()
    for o in range(1, shards):
        place(lax.rem(me + o, shards)).start()
    for o in range(1, shards):
        peer = lax.rem(me + o, shards)
        across_slab(peer, peer).wait_recv()
    whole = sbuf[0]
    for i in range(1, shards):
        whole = whole + sbuf[i]

    lane_e = lax.broadcasted_iota(jnp.int32, (lanes, chan), 0)
    channel_e = lax.broadcasted_iota(jnp.int32, (lanes, chan), 1)

    def spread(matrix):
        return jnp.dot(whole, matrix, precision=HIGH, preferred_element_type=F32)

    for copy in params:
        copy.wait()
    cnt = spread((lane_e == 2 * GROUPS).astype(F32))
    mean = spread(member(channel_e, lane_e, 0)) / cnt
    var = spread(member(channel_e, lane_e, GROUPS)) / cnt - mean * mean
    scale = rows_v[0] * (1.0 / jnp.sqrt(var + 1e-05))

    for copy, _, receives in halos:

        @pl.when(receives)
        def _(copy=copy):
            copy.wait_recv()

    @pl.when(me == 0)
    def _():
        idtab[pl.ds(0, LEAD), :] = jnp.full((LEAD, chan), -1, jnp.int32)

    ids = idtab[...]
    frame_mean = jnp.zeros(ids.shape, F32)
    frame_scale = jnp.zeros(ids.shape, F32)
    for c in range(CLIPS):
        frame_mean = jnp.where(ids == c, mean[c : c + 1, :], frame_mean)
        frame_scale = jnp.where(ids == c, scale[c : c + 1, :], frame_scale)
    mean_t[...] = frame_mean
    scale_t[...] = frame_scale

    shift = rows_v[1]
    bsp = rows_v[2]
    btm = rows_v[3]
    column = lax.broadcasted_iota(jnp.int32, (width, chan), 0)

    def normalise(f, place_at):
        mu = mean_t[pl.ds(f + LEAD - BACK, 1), :]
        sc = scale_t[pl.ds(f + LEAD - BACK, 1), :]
        for i in range(band + 2):
            x = xin[f, pl.ds(i * width, width), :].astype(F32)
            v = (x - mu) * sc + shift
            half = 0.5 * v
            y = half + half * jnp.tanh(half)
            if i == 0:
                y = jnp.where(row > 0, y, 0.0)
            if i == band + 1:
                y = jnp.where(row < bands - 1, y, 0.0)
            left = jnp.where(column == 0, 0.0, pltpu.roll(y, 1, 0))
            right = jnp.where(column == width - 1, 0.0, pltpu.roll(y, width - 1, 0))
            nbuf[i, place_at, :, pl.ds(0, chan)] = left.astype(BF16)
            nbuf[i, place_at, :, pl.ds(chan, chan)] = y.astype(BF16)
            nbuf[i, place_at, :, pl.ds(2 * chan, chan)] = right.astype(BF16)

    def convolve(entry):
        size = band * group * width
        acc = jnp.zeros((size, chan), F32) + bsp
        for a in range(3):
            acc = acc + jnp.dot(
                nbuf[pl.ds(a, band)].reshape(size, 3 * chan),
                wsp_ref[a],
                preferred_element_type=F32,
            )
        out = acc.astype(BF16).reshape(band, group, width, chan)
        for i in range(band):
            for g in range(group):
                spat[entry + g, pl.ds(i * width, width), :] = out[i, g]

    def slot_frame(slot, entry):
        t = order_ref[slot]
        now = idtab[pl.ds(t + LEAD, 1), :]
        acc = xin[t + BACK, pl.ds(width, cells), :].astype(F32) + btm
        for k in range(BACK + 1):
            term = jnp.dot(spat[entry(t, k)], wtm_ref[k], preferred_element_type=F32)
            if k > 0:
                same = idtab[pl.ds(t + LEAD - k, 1), :] == now
                term = jnp.where(same, term, 0.0)
            acc = acc + term
        sendbuf[slot] = acc.astype(BF16)

    def exchange(d, src, q):
        return pltpu.make_async_remote_copy(
            src_ref=sendbuf.at[d * per_peer + q],
            dst_ref=got_ref.at[src * per_peer + q],
            send_sem=x_send.at[d * per_peer + q],
            recv_sem=x_recv.at[src * per_peer + q],
            device_id=(d, row),
            device_id_type=MESH,
        )

    slots = (shards - 1) * per_peer
    far = shards // 2 * per_peer

    def target(i):
        if per_peer <= 2:
            inside = 1 - i // (slots // 2 * 2)
            i = i + inside * lax.rem(row, 2) * (1 - 2 * lax.rem(i, 2))
            i = i // 2 + (1 - lax.rem(i, 2)) * (far - 1)
        return flipped(me, shards - 1 - i // per_peer, shards), lax.rem(i, per_peer)

    @pl.loop(0, direct)
    def _(i):
        d, q = target(i)
        slot = d * per_peer + q

        @pl.loop(0, BACK + 1)
        def _(k):
            normalise(order_ref[slot] + BACK - k, k)

        convolve(count + BACK)

        slot_frame(slot, lambda t, k: count + BACK + k)
        exchange(d, me, q).start()

    @pl.loop(0, (count + BACK) // group)
    def _(g):
        @pl.loop(0, group)
        def _(k):
            normalise(g * group + k, k)

        convolve(g * group)

    @pl.loop(direct, (shards - 1) * per_peer)
    def _(i):
        d, q = target(i)
        slot_frame(d * per_peer + q, lambda t, k: t + BACK - k)
        exchange(d, me, q).start()

    def keep(q):
        return pltpu.make_async_copy(
            sendbuf.at[me * per_peer + q], got_ref.at[me * per_peer + q], own_sem.at[q]
        )

    keep_pos = pltpu.make_async_copy(pos_ref.at[me], gotpos_ref.at[me], own_sem.at[per_peer])
    keep_pos.start()
    for q in range(per_peer):
        slot_frame(me * per_peer + q, lambda t, k: t + BACK - k)
        keep(q).start()

    for copy, sends, _ in halos:

        @pl.when(sends)
        def _(copy=copy):
            copy.wait_send()

    for o in range(1, bands):
        across_rows(lax.rem(row + o, bands), row).wait_send()
    for o in range(1, shards):
        across_slab(lax.rem(me + o, shards), me).wait_send()
    for o in range(1, shards):
        peer = lax.rem(me + o, shards)
        place(peer).wait_send()
        pltpu.make_async_remote_copy(
            src_ref=pos_ref.at[peer],
            dst_ref=gotpos_ref.at[peer],
            send_sem=p_send.at[peer],
            recv_sem=p_recv.at[peer],
            device_id=(peer, row),
            device_id_type=MESH,
        ).wait_recv()
    keep_pos.wait()
    for q in range(per_peer):
        keep(q).wait()

    @pl.loop(0, (shards - 1) * per_peer)
    def _(i):
        d, q = target(i)
        exchange(d, me, q).wait_send()
        exchange(d, d, q).wait_recv()


def lift_kernel(pos_ref, x_hbm, w_hbm, o_hbm, x, w, out, x_sem, w_sem, out_sem):
    count = x.shape[0]
    per_peer = count // pos_ref.shape[0]

    def load(s):
        return pltpu.make_async_copy(x_hbm.at[s], x.at[s], x_sem.at[s])

    def store(s):
        p = pos_ref[s // per_peer, 0, lax.rem(s, per_peer)]
        return pltpu.make_async_copy(out.at[s], o_hbm.at[p], out_sem.at[s])

    weights = pltpu.make_async_copy(w_hbm, w, w_sem)
    weights.start()

    @pl.loop(0, count)
    def _(s):
        load(s).start()

    weights.wait()

    @pl.loop(0, count)
    def _(s):
        load(s).wait()
        out[s] = jnp.dot(x[s], w[...], preferred_element_type=F32).astype(BF16)
        store(s).start()

    @pl.loop(0, count)
    def _(s):
        store(s).wait()


def route(pack_dest, shards):
    count = pack_dest.shape[0]
    per_peer = count // shards
    target = pack_dest // count
    index = jnp.arange(count, dtype=jnp.int32)
    earlier = jnp.logical_and(target[:, None] == target[None, :], index[:, None] < index[None, :])
    slot_of = target * per_peer + jnp.sum(earlier.astype(jnp.int32), axis=0)
    selector = (slot_of[None, :] == index[:, None]).astype(jnp.int32)
    order = jnp.sum(selector * index[None, :], axis=1)
    position = jnp.sum(selector * (pack_dest % count)[None, :], axis=1)
    return order, position


def body(
    frames, clip_ids, norm_gain, norm_shift, w_spatial, b_spatial, w_time, b_time, w_lift, pack_dest
):
    count, band, width, chan = frames.shape
    lifted = w_lift.shape[1]
    cells = band * width
    shards = lax.axis_size("slab")
    bands = lax.axis_size("rows")
    per_peer = count // shards
    order, position = route(pack_dest, shards)
    smem = pl.BlockSpec(memory_space=pltpu.SMEM)
    hbm = pl.BlockSpec(memory_space=pl.ANY)
    dma = pltpu.SemaphoreType.DMA
    got, gotpos = pl.pallas_call(
        functools.partial(block_kernel, shards, bands, width),
        out_shape=(
            jax.ShapeDtypeStruct((count, cells, chan), BF16),
            jax.ShapeDtypeStruct((shards, 1, 128), jnp.int32),
        ),
        in_specs=[smem] * 3 + [hbm] * 7,
        out_specs=(hbm, hbm),
        scratch_shapes=[
            pltpu.VMEM((count + BACK, cells + 2 * width, chan), BF16),
            pltpu.VMEM((shards, 1, 128), jnp.int32),
            pltpu.VMEM((LEAD + count, chan), jnp.int32),
            pltpu.VMEM((LEAD + count, chan), F32),
            pltpu.VMEM((LEAD + count, chan), F32),
            pltpu.VMEM((band + 2, BACK + 1, width, 3 * chan), BF16),
            pltpu.VMEM((count + 2 * BACK + 1, cells, chan), BF16),
            pltpu.VMEM((count, cells, chan), BF16),
            pltpu.VMEM((bands, CLIPS, 128), F32),
            pltpu.VMEM((shards, CLIPS, 128), F32),
            pltpu.VMEM((4, 1, chan), F32),
            pltpu.VMEM((3, 3 * chan, chan), BF16),
            pltpu.VMEM((BACK + 1, chan, chan), BF16),
            dma((count,)),
            dma((6,)),
            dma((6,)),
            dma((6,)),
            dma((bands,)),
            dma((bands,)),
            dma((shards,)),
            dma((shards,)),
            dma((shards,)),
            dma((shards,)),
            dma((count,)),
            dma((count,)),
            dma((per_peer + 1,)),
        ],
        compiler_params=pltpu.CompilerParams(
            collective_id=0, has_side_effects=True, vmem_limit_bytes=60 * 1024 * 1024
        ),
        name="block",
    )(
        order,
        position,
        clip_ids,
        frames.reshape(count, cells, chan),
        norm_gain.reshape(1, chan),
        norm_shift.reshape(1, chan),
        b_spatial.reshape(1, chan),
        b_time.reshape(1, chan),
        w_spatial.reshape(3, 3 * chan, chan),
        w_time,
    )
    packed = pl.pallas_call(
        lift_kernel,
        out_shape=jax.ShapeDtypeStruct((count, cells, lifted), BF16),
        in_specs=[smem, hbm, hbm],
        out_specs=hbm,
        scratch_shapes=[
            pltpu.VMEM((count, cells, chan), BF16),
            pltpu.VMEM((chan, lifted), BF16),
            pltpu.VMEM((count, cells, lifted), BF16),
            dma((count,)),
            dma,
            dma((count,)),
        ],
        compiler_params=pltpu.CompilerParams(vmem_limit_bytes=60 * 1024 * 1024),
        name="lift",
    )(gotpos, got, w_lift)
    return packed.reshape(count, band, width, lifted)


def solution(mesh):
    in_specs = (
        P("slab", "rows", None, None),
        P("slab"),
        P(),
        P(),
        P(),
        P(),
        P(),
        P(),
        P(),
        P("slab"),
    )
    out_specs = P("slab", "rows", None, None)
    return jax.shard_map(body, mesh=mesh, in_specs=in_specs, out_specs=out_specs, check_vma=False)
```

```python
import functools

import jax
import jax.numpy as jnp
from jax import lax
from jax.experimental import pallas as pl
from jax.experimental.pallas import tpu as pltpu
from jax.sharding import PartitionSpec as P

GROUPS = 32
CLIPS = 16
BACK = 2
LEAD = 8
DIRECT = 5
MESH = pl.DeviceIdType.MESH
HIGH = lax.Precision.HIGHEST
F32 = jnp.float32
BF16 = jnp.bfloat16


def flipped(index, mask, count):
    out, bit = 0, 1
    while bit < count:
        out = out + lax.rem(lax.rem(index // bit, 2) + lax.rem(mask // bit, 2), 2) * bit
        bit *= 2
    return out


def block_kernel(
    shards,
    bands,
    width,
    order_ref,
    position_ref,
    clip_ref,
    frames_ref,
    gain_hbm,
    shift_hbm,
    bsp_hbm,
    btm_hbm,
    wsp_hbm,
    wtm_hbm,
    got_ref,
    gotpos_ref,
    xin,
    pos_ref,
    idtab,
    mean_t,
    scale_t,
    nbuf,
    spat,
    sendbuf,
    rbuf,
    sbuf,
    rows_v,
    wsp_ref,
    wtm_ref,
    load_sem,
    param_sem,
    halo_send,
    halo_recv,
    r_send,
    r_recv,
    s_send,
    s_recv,
    p_send,
    p_recv,
    x_send,
    x_recv,
    own_sem,
):
    count, cells, chan = frames_ref.shape
    per_peer = count // shards
    per_group = chan // GROUPS
    band = cells // width
    me = lax.axis_index("slab")
    row = lax.axis_index("rows")
    group = BACK + 1
    direct = min(DIRECT, (shards - 1) * per_peer)

    def load(t):
        return pltpu.make_async_copy(
            frames_ref.at[t], xin.at[t + BACK, pl.ds(width, cells)], load_sem.at[t]
        )

    @pl.loop(0, count)
    def _(t):
        load(t).start()

    params = [
        pltpu.make_async_copy(src, dst, param_sem.at[i])
        for i, (src, dst) in enumerate(
            (
                (gain_hbm, rows_v.at[0]),
                (shift_hbm, rows_v.at[1]),
                (bsp_hbm, rows_v.at[2]),
                (btm_hbm, rows_v.at[3]),
                (wsp_hbm, wsp_ref),
                (wtm_hbm, wtm_ref),
            )
        )
    ]
    for copy in params:
        copy.start()

    barrier = pltpu.get_barrier_semaphore()
    for o in range(1, bands):
        pl.semaphore_signal(
            barrier, inc=1, device_id=(me, lax.rem(row + o, bands)), device_id_type=MESH
        )
    for o in range(1, shards):
        pl.semaphore_signal(
            barrier, inc=1, device_id=(lax.rem(me + o, shards), row), device_id_type=MESH
        )

    for t in range(count):
        idtab[LEAD + t : LEAD + t + 1, :] = jnp.full((1, chan), clip_ref[t], jnp.int32)
    pos_lane = lax.broadcasted_iota(jnp.int32, (1, 128), 1)
    for d in range(shards):
        line = jnp.zeros((1, 128), jnp.int32)
        for q in range(per_peer):
            line = jnp.where(pos_lane == q, position_ref[d * per_peer + q], line)
        pos_ref[d] = line
    pl.semaphore_wait(barrier, bands - 1 + shards - 1)

    top = pl.ds(0, width)
    bottom = pl.ds(width + cells, width)
    first = pl.ds(0, width)
    last = pl.ds(cells - width, width)
    own = pl.ds(BACK, count)
    tail = pl.ds(count - BACK, BACK)
    prior = pl.ds(0, BACK)
    up_slab = lax.rem(me + 1, shards)
    up_row = lax.rem(row + 1, bands)
    down_row = lax.rem(row + bands - 1, bands)

    def halo(i, src, dst, slab, band_index):
        return pltpu.make_async_remote_copy(
            src_ref=src,
            dst_ref=dst,
            send_sem=halo_send.at[i],
            recv_sem=halo_recv.at[i],
            device_id=(slab, band_index),
            device_id_type=MESH,
        )

    halos = (
        (
            halo(0, frames_ref.at[tail], xin.at[prior, pl.ds(width, cells)], up_slab, row),
            me < shards - 1,
            me > 0,
        ),
        (
            halo(1, xin.at[prior, pl.ds(cells, width)], xin.at[prior, top], me, up_row),
            jnp.logical_and(me > 0, row < bands - 1),
            jnp.logical_and(me > 0, row > 0),
        ),
        (
            halo(2, xin.at[prior, pl.ds(width, width)], xin.at[prior, bottom], me, down_row),
            jnp.logical_and(me > 0, row > 0),
            jnp.logical_and(me > 0, row < bands - 1),
        ),
        (
            halo(3, frames_ref.at[:, last], xin.at[own, top], me, up_row),
            row < bands - 1,
            row > 0,
        ),
        (
            halo(4, frames_ref.at[:, first], xin.at[own, bottom], me, down_row),
            row > 0,
            row < bands - 1,
        ),
        (
            halo(5, idtab.at[pl.ds(count, LEAD)], idtab.at[pl.ds(0, LEAD)], up_slab, row),
            me < shards - 1,
            me > 0,
        ),
    )
    for copy, sends, _ in halos[:1] + halos[3:]:

        @pl.when(sends)
        def _(copy=copy):
            copy.start()

    def place(d):
        return pltpu.make_async_remote_copy(
            src_ref=pos_ref.at[d],
            dst_ref=gotpos_ref.at[me],
            send_sem=p_send.at[d],
            recv_sem=p_recv.at[me],
            device_id=(d, row),
            device_id_type=MESH,
        )

    clip_row = lax.broadcasted_iota(jnp.int32, (CLIPS, chan), 0)
    zero = jnp.zeros((CLIPS, chan), F32)

    def stats(t, carry):
        total, squares, number = carry
        load(t).wait()
        x = xin[t + BACK, pl.ds(width, cells), :].astype(F32)
        one = jnp.sum(x, axis=0, keepdims=True)
        two = jnp.sum(x * x, axis=0, keepdims=True)
        mine = clip_row == idtab[pl.ds(t + LEAD, 1), :]
        return (
            total + jnp.where(mine, one, 0.0),
            squares + jnp.where(mine, two, 0.0),
            number + jnp.where(mine, 1.0, 0.0),
        )

    total, squares, number = lax.fori_loop(0, count, stats, (zero, zero, zero))
    lanes = 128
    channel = lax.broadcasted_iota(jnp.int32, (chan, lanes), 0)
    lane = lax.broadcasted_iota(jnp.int32, (chan, lanes), 1)

    def member(channel, lane, start):
        low = (lane - start) * per_group
        return jnp.logical_and(channel >= low, channel < low + per_group).astype(F32)

    table = jnp.dot(
        total, member(channel, lane, 0), precision=HIGH, preferred_element_type=F32
    ) + jnp.dot(
        squares, member(channel, lane, GROUPS), precision=HIGH, preferred_element_type=F32
    )
    lane_c = lax.broadcasted_iota(jnp.int32, (CLIPS, lanes), 1)
    table = jnp.where(lane_c == 2 * GROUPS, number[:, :lanes] * float(cells * per_group), table)

    rbuf[row] = table

    def across_rows(peer, src):
        return pltpu.make_async_remote_copy(
            src_ref=rbuf.at[src],
            dst_ref=rbuf.at[src],
            send_sem=r_send.at[peer],
            recv_sem=r_recv.at[src],
            device_id=(me, peer),
            device_id_type=MESH,
        )

    for o in range(1, bands):
        across_rows(lax.rem(row + o, bands), row).start()
    for o in range(1, bands):
        peer = lax.rem(row + o, bands)
        across_rows(peer, peer).wait_recv()
    part = rbuf[0]
    for i in range(1, bands):
        part = part + rbuf[i]
    sbuf[me] = part

    def across_slab(peer, src):
        return pltpu.make_async_remote_copy(
            src_ref=sbuf.at[src],
            dst_ref=sbuf.at[src],
            send_sem=s_send.at[peer],
            recv_sem=s_recv.at[src],
            device_id=(peer, row),
            device_id_type=MESH,
        )

    for o in range(1, shards):
        across_slab(lax.rem(me + o, shards), me).start()
    for o in range(1, shards):
        place(lax.rem(me + o, shards)).start()
    for o in range(1, shards):
        peer = lax.rem(me + o, shards)
        across_slab(peer, peer).wait_recv()
    whole = sbuf[0]
    for i in range(1, shards):
        whole = whole + sbuf[i]

    lane_e = lax.broadcasted_iota(jnp.int32, (lanes, chan), 0)
    channel_e = lax.broadcasted_iota(jnp.int32, (lanes, chan), 1)

    def spread(matrix):
        return jnp.dot(whole, matrix, precision=HIGH, preferred_element_type=F32)

    for copy in params:
        copy.wait()
    cnt = spread((lane_e == 2 * GROUPS).astype(F32))
    mean = spread(member(channel_e, lane_e, 0)) / cnt
    var = spread(member(channel_e, lane_e, GROUPS)) / cnt - mean * mean
    scale = rows_v[0] * (1.0 / jnp.sqrt(var + 1e-05))

    @pl.when(me > 0)
    def _():
        halos[0][0].wait_recv()

    for copy, sends, _ in halos[1:3]:

        @pl.when(sends)
        def _(copy=copy):
            copy.start()

    for copy, _, receives in halos[1:]:

        @pl.when(receives)
        def _(copy=copy):
            copy.wait_recv()

    @pl.when(me == 0)
    def _():
        idtab[pl.ds(0, LEAD), :] = jnp.full((LEAD, chan), -1, jnp.int32)

    ids = idtab[...]
    frame_mean = jnp.zeros(ids.shape, F32)
    frame_scale = jnp.zeros(ids.shape, F32)
    for c in range(CLIPS):
        frame_mean = jnp.where(ids == c, mean[c : c + 1, :], frame_mean)
        frame_scale = jnp.where(ids == c, scale[c : c + 1, :], frame_scale)
    mean_t[...] = frame_mean
    scale_t[...] = frame_scale

    shift = rows_v[1]
    bsp = rows_v[2]
    btm = rows_v[3]
    column = lax.broadcasted_iota(jnp.int32, (width, chan), 0)

    def normalise(f, place_at):
        mu = mean_t[pl.ds(f + LEAD - BACK, 1), :]
        sc = scale_t[pl.ds(f + LEAD - BACK, 1), :]
        for i in range(band + 2):
            x = xin[f, pl.ds(i * width, width), :].astype(F32)
            v = (x - mu) * sc + shift
            half = 0.5 * v
            y = half + half * jnp.tanh(half)
            if i == 0:
                y = jnp.where(row > 0, y, 0.0)
            if i == band + 1:
                y = jnp.where(row < bands - 1, y, 0.0)
            left = jnp.where(column == 0, 0.0, pltpu.roll(y, 1, 0))
            right = jnp.where(column == width - 1, 0.0, pltpu.roll(y, width - 1, 0))
            nbuf[i, place_at, :, pl.ds(0, chan)] = left.astype(BF16)
            nbuf[i, place_at, :, pl.ds(chan, chan)] = y.astype(BF16)
            nbuf[i, place_at, :, pl.ds(2 * chan, chan)] = right.astype(BF16)

    def convolve(entry):
        size = band * group * width
        acc = jnp.zeros((size, chan), F32) + bsp
        for a in range(3):
            acc = acc + jnp.dot(
                nbuf[pl.ds(a, band)].reshape(size, 3 * chan),
                wsp_ref[a],
                preferred_element_type=F32,
            )
        out = acc.astype(BF16).reshape(band, group, width, chan)
        for i in range(band):
            for g in range(group):
                spat[entry + g, pl.ds(i * width, width), :] = out[i, g]

    def slot_frame(slot, entry):
        t = order_ref[slot]
        now = idtab[pl.ds(t + LEAD, 1), :]
        acc = xin[t + BACK, pl.ds(width, cells), :].astype(F32) + btm
        for k in range(BACK + 1):
            term = jnp.dot(spat[entry(t, k)], wtm_ref[k], preferred_element_type=F32)
            if k > 0:
                same = idtab[pl.ds(t + LEAD - k, 1), :] == now
                term = jnp.where(same, term, 0.0)
            acc = acc + term
        sendbuf[slot] = acc.astype(BF16)

    def exchange(d, src, q):
        return pltpu.make_async_remote_copy(
            src_ref=sendbuf.at[d * per_peer + q],
            dst_ref=got_ref.at[src * per_peer + q],
            send_sem=x_send.at[d * per_peer + q],
            recv_sem=x_recv.at[src * per_peer + q],
            device_id=(d, row),
            device_id_type=MESH,
        )

    slots = (shards - 1) * per_peer
    far = shards // 2 * per_peer

    rounds = far - direct
    if far + 2 * rounds > slots:
        rounds = 0

    def target(u):
        return flipped(me, shards - 1 - u // per_peer, shards), lax.rem(u, per_peer)

    def mixed(i):
        odd = lax.rem(row, 2)
        g, h = i // 3, lax.rem(i, 3)
        is_far = (1 - odd) * ((2 - h) // 2) + odd * lax.rem(h, 2)
        near = far + 2 * g + (1 - odd) * (h - 1) + odd * (h // 2)
        return is_far * (direct + g) + (1 - is_far) * near

    @pl.loop(0, direct)
    def _(i):
        d, q = target(i)
        slot = d * per_peer + q

        @pl.loop(0, BACK + 1)
        def _(k):
            normalise(order_ref[slot] + BACK - k, k)

        convolve(count + BACK)

        slot_frame(slot, lambda t, k: count + BACK + k)
        exchange(d, me, q).start()

    @pl.loop(0, (count + BACK) // group)
    def _(g):
        @pl.loop(0, group)
        def _(k):
            normalise(g * group + k, k)

        convolve(g * group)

    def send(u):
        d, q = target(u)
        slot_frame(d * per_peer + q, lambda t, k: t + BACK - k)
        exchange(d, me, q).start()

    @pl.loop(0, slots - direct)
    def _(i):
        if rounds:
            inside = 1 - i // (3 * rounds)
            send(inside * mixed(inside * i) + (1 - inside) * (direct + i))
        else:
            send(direct + i)

    def keep(q):
        return pltpu.make_async_copy(
            sendbuf.at[me * per_peer + q], got_ref.at[me * per_peer + q], own_sem.at[q]
        )

    keep_pos = pltpu.make_async_copy(pos_ref.at[me], gotpos_ref.at[me], own_sem.at[per_peer])
    keep_pos.start()
    for q in range(per_peer):
        slot_frame(me * per_peer + q, lambda t, k: t + BACK - k)
        keep(q).start()

    for copy, sends, _ in halos:

        @pl.when(sends)
        def _(copy=copy):
            copy.wait_send()

    for o in range(1, bands):
        across_rows(lax.rem(row + o, bands), row).wait_send()
    for o in range(1, shards):
        across_slab(lax.rem(me + o, shards), me).wait_send()
    for o in range(1, shards):
        peer = lax.rem(me + o, shards)
        place(peer).wait_send()
        pltpu.make_async_remote_copy(
            src_ref=pos_ref.at[peer],
            dst_ref=gotpos_ref.at[peer],
            send_sem=p_send.at[peer],
            recv_sem=p_recv.at[peer],
            device_id=(peer, row),
            device_id_type=MESH,
        ).wait_recv()
    keep_pos.wait()
    for q in range(per_peer):
        keep(q).wait()

    @pl.loop(0, (shards - 1) * per_peer)
    def _(i):
        d, q = target(i)
        exchange(d, me, q).wait_send()
        exchange(d, d, q).wait_recv()


def lift_kernel(pos_ref, x_hbm, w_hbm, o_hbm, x, w, out, x_sem, w_sem, out_sem):
    count = x.shape[0]
    per_peer = count // pos_ref.shape[0]

    def load(s):
        return pltpu.make_async_copy(x_hbm.at[s], x.at[s], x_sem.at[s])

    def store(s):
        p = pos_ref[s // per_peer, 0, lax.rem(s, per_peer)]
        return pltpu.make_async_copy(out.at[s], o_hbm.at[p], out_sem.at[s])

    weights = pltpu.make_async_copy(w_hbm, w, w_sem)
    weights.start()

    @pl.loop(0, count)
    def _(s):
        load(s).start()

    weights.wait()

    @pl.loop(0, count)
    def _(s):
        load(s).wait()
        out[s] = jnp.dot(x[s], w[...], preferred_element_type=F32).astype(BF16)
        store(s).start()

    @pl.loop(0, count)
    def _(s):
        store(s).wait()


def route(pack_dest, shards):
    count = pack_dest.shape[0]
    per_peer = count // shards
    target = pack_dest // count
    index = jnp.arange(count, dtype=jnp.int32)
    earlier = jnp.logical_and(target[:, None] == target[None, :], index[:, None] < index[None, :])
    slot_of = target * per_peer + jnp.sum(earlier.astype(jnp.int32), axis=0)
    selector = (slot_of[None, :] == index[:, None]).astype(jnp.int32)
    order = jnp.sum(selector * index[None, :], axis=1)
    position = jnp.sum(selector * (pack_dest % count)[None, :], axis=1)
    return order, position


def body(
    frames, clip_ids, norm_gain, norm_shift, w_spatial, b_spatial, w_time, b_time, w_lift, pack_dest
):
    count, band, width, chan = frames.shape
    lifted = w_lift.shape[1]
    cells = band * width
    shards = lax.axis_size("slab")
    bands = lax.axis_size("rows")
    per_peer = count // shards
    order, position = route(pack_dest, shards)
    smem = pl.BlockSpec(memory_space=pltpu.SMEM)
    hbm = pl.BlockSpec(memory_space=pl.ANY)
    dma = pltpu.SemaphoreType.DMA
    got, gotpos = pl.pallas_call(
        functools.partial(block_kernel, shards, bands, width),
        out_shape=(
            jax.ShapeDtypeStruct((count, cells, chan), BF16),
            jax.ShapeDtypeStruct((shards, 1, 128), jnp.int32),
        ),
        in_specs=[smem] * 3 + [hbm] * 7,
        out_specs=(hbm, hbm),
        scratch_shapes=[
            pltpu.VMEM((count + BACK, cells + 2 * width, chan), BF16),
            pltpu.VMEM((shards, 1, 128), jnp.int32),
            pltpu.VMEM((LEAD + count, chan), jnp.int32),
            pltpu.VMEM((LEAD + count, chan), F32),
            pltpu.VMEM((LEAD + count, chan), F32),
            pltpu.VMEM((band + 2, BACK + 1, width, 3 * chan), BF16),
            pltpu.VMEM((count + 2 * BACK + 1, cells, chan), BF16),
            pltpu.VMEM((count, cells, chan), BF16),
            pltpu.VMEM((bands, CLIPS, 128), F32),
            pltpu.VMEM((shards, CLIPS, 128), F32),
            pltpu.VMEM((4, 1, chan), F32),
            pltpu.VMEM((3, 3 * chan, chan), BF16),
            pltpu.VMEM((BACK + 1, chan, chan), BF16),
            dma((count,)),
            dma((6,)),
            dma((6,)),
            dma((6,)),
            dma((bands,)),
            dma((bands,)),
            dma((shards,)),
            dma((shards,)),
            dma((shards,)),
            dma((shards,)),
            dma((count,)),
            dma((count,)),
            dma((per_peer + 1,)),
        ],
        compiler_params=pltpu.CompilerParams(
            collective_id=0, has_side_effects=True, vmem_limit_bytes=60 * 1024 * 1024
        ),
        name="block",
    )(
        order,
        position,
        clip_ids,
        frames.reshape(count, cells, chan),
        norm_gain.reshape(1, chan),
        norm_shift.reshape(1, chan),
        b_spatial.reshape(1, chan),
        b_time.reshape(1, chan),
        w_spatial.reshape(3, 3 * chan, chan),
        w_time,
    )
    packed = pl.pallas_call(
        lift_kernel,
        out_shape=jax.ShapeDtypeStruct((count, cells, lifted), BF16),
        in_specs=[smem, hbm, hbm],
        out_specs=hbm,
        scratch_shapes=[
            pltpu.VMEM((count, cells, chan), BF16),
            pltpu.VMEM((chan, lifted), BF16),
            pltpu.VMEM((count, cells, lifted), BF16),
            dma((count,)),
            dma,
            dma((count,)),
        ],
        compiler_params=pltpu.CompilerParams(vmem_limit_bytes=60 * 1024 * 1024),
        name="lift",
    )(gotpos, got, w_lift)
    return packed.reshape(count, band, width, lifted)


def solution(mesh):
    in_specs = (
        P("slab", "rows", None, None),
        P("slab"),
        P(),
        P(),
        P(),
        P(),
        P(),
        P(),
        P(),
        P("slab"),
    )
    out_specs = P("slab", "rows", None, None)
    return jax.shard_map(body, mesh=mesh, in_specs=in_specs, out_specs=out_specs, check_vma=False)
```
